32 devices in a mesh: gx: 4 (over x, core), gy: 4 (over z), gz: 2 (over y).
Axes of the slice: x: 2, y: 2, z: 4, core: 2. Of those that a mesh axis runs over, the one named last changes fastest.
Arguments:
- gram_factor: bfloat16 [384, 384, 384], P(('gx', 'gy', 'gz')), may hold values from -0.3125 to 0.3125
- coupling: bfloat16 [384, 384, 128], P(('gx', 'gy', 'gz')), may hold values from -0.375 to 0.375
- order_class: int32 [384], P(('gx', 'gy', 'gz')), may hold values from 0 to 2
- first_moves: int32 [96], P(('gx', 'gy', 'gz')), may hold values from 0 to 11, as said below
- second_moves: int32 [96], P(('gx', 'gy', 'gz')), may hold values from 0 to 11, as said below
- trace_index: int32 [384, 128], P(('gx', 'gy', 'gz')), may hold values from 1 to 322, as said below
- owner_index: int32 [384, 128], P(('gx', 'gy', 'gz')), may hold values from 0 to 255
- traces: bfloat16 [64, 4, 32, 256], P('gx', 'gy', 'gz'), may hold values from -6 to 6
Outputs:
- applied: float32 [64, 4, 32, 256], P('gx', 'gy', 'gz')
The draws below stay inside these ranges and needn't reach their ends.
Inputs may be any that keep to these rules, and one draw needn't show every extreme that they name: `first_moves`: on each device the 3 entries are distinct slots. `second_moves`: on each device the 3 entries are distinct slots. `trace_index`: never a corner cell of the extended grid.
All inputs are finite; a program needn't handle non-finite values.
Results may differ from the reference program's by a relative error of at most 0.0044.
Values may be sent and summed in bfloat16 or wider, within the bound.
A program may use at most 64 MiB of HBM per device.

```python
import jax
import jax.numpy as jnp
from jax import lax

W = 384
K = 128
R = 256
FX = 16
FZ = 16
E_DEV = 12
M = 3
NDEV = 32
ELEMS = 384
NXT = 64
NZT = 32
N_GX = 4
N_GY = 4
N_GZ = 2


def slot_lists(key):
    keys = jax.random.split(key, NDEV)
    picks = jax.vmap(lambda single: jax.random.permutation(single, E_DEV)[:M])(keys)
    return picks.reshape(-1).astype(jnp.int32)


def draw_first_moves(key, part):
    return slot_lists(jax.random.fold_in(key, 1))


def draw_second_moves(key, part):
    return slot_lists(jax.random.fold_in(key, 2))


def draw_trace_index(key, part):
    middle = FX * (FZ + 2)
    choice_cells = jax.random.randint(jax.random.fold_in(key, 3), (NDEV * E_DEV, K), 0, middle + 2 * FZ)
    inner = (1 + choice_cells // (FZ + 2)) * (FZ + 2) + choice_cells % (FZ + 2)
    edge = choice_cells - middle
    edge_row = jnp.where(edge < FZ, 0, FX + 1)
    outer = edge_row * (FZ + 2) + 1 + edge % FZ
    return jnp.where(choice_cells < middle, inner, outer).astype(jnp.int32)


def set_ends(values, stream_key, least, largest):
    longest = values.shape.index(max(values.shape))
    spots = []
    for shift in (0, 1):
        where = [jax.random.randint(jax.random.fold_in(stream_key, axis), (), 0, length) for axis, length in enumerate(values.shape)]
        where[longest] = (where[longest] + shift) % values.shape[longest]
        spots.append(tuple(where))
    return values.at[spots[0]].set(least).at[spots[1]].set(largest)


def levels(stream_key, shape, pieces, low, top_value):
    loudness, own = 1.0, jax.random.fold_in(stream_key, 6)
    for dim, parts in pieces:
        draws = jnp.exp(jax.random.uniform(jax.random.fold_in(own, dim), (parts,), jnp.float32, low / len(pieces), top_value / len(pieces)))
        loudness = loudness * jnp.repeat(draws, shape[dim] // parts).reshape([-1 if axis == dim else 1 for axis in range(len(shape))])
    return loudness


def normal_values(key, shape, width, reach, pieces=(), kind=jnp.bfloat16):
    level = levels(key, shape, pieces, -0.22, 0.18) if pieces else 1.0
    drawn = jax.random.normal(key, shape, jnp.float32) * width * level
    return jnp.minimum(jnp.maximum(drawn, -reach), reach).astype(kind)


def setup_inputs(seed: int = 0) -> dict:
    key_list = jax.random.split(jax.random.key(seed), 9)
    gram_factor = normal_values(key_list[0], (ELEMS, W, W), W ** -0.5, 0.3125, ((0, 32),))
    coupling = normal_values(key_list[1], (ELEMS, W, K), (2 * K) ** -0.5, 0.375, ((0, 32),))
    order_class = set_ends(jax.random.randint(key_list[2], (ELEMS,), 0, 3), jax.random.fold_in(key_list[2], 1), 0, 2).astype(jnp.int32)
    first_moves = draw_first_moves(jax.random.fold_in(key_list[8], 71), 0)
    second_moves = draw_second_moves(jax.random.fold_in(key_list[8], 71), 0)
    trace_index = draw_trace_index(jax.random.fold_in(key_list[8], 71), 0)
    owner_index = set_ends(jax.random.randint(key_list[6], (ELEMS, K), 0, FX * FZ), jax.random.fold_in(key_list[6], 1), 0, (FX * FZ) - 1).astype(jnp.int32)
    traces = normal_values(key_list[7], (NXT, N_GY, NZT, R), 1.0, 6.0, ((0, 4), (1, 4), (2, 2)))
    return dict(gram_factor=gram_factor, coupling=coupling, order_class=order_class, first_moves=first_moves, second_moves=second_moves, trace_index=trace_index, owner_index=owner_index, traces=traces)


def element_products(gram_factor, coupling, order_class):
    rows = jnp.arange(W, dtype=jnp.int32)
    widths = (W * (2 + order_class)) // 4
    keep = (rows[None, :] < widths[:, None]).astype(gram_factor.dtype)
    masked = gram_factor * keep[:, :, None]
    def one_element(pair):
        return jnp.dot(pair[0], pair[1], preferred_element_type=jnp.float32).astype(jnp.bfloat16)
    return lax.map(one_element, (masked, coupling))


def relocate(first_moves, second_moves):
    device_ids = jnp.arange(NDEV, dtype=jnp.int32)
    layout = jnp.arange(NDEV * E_DEV, dtype=jnp.int32).reshape(NDEV, E_DEV)
    first_slots = first_moves.reshape(NDEV, M)
    partner = device_ids ^ 1
    layout = layout.at[device_ids[:, None], first_slots].set(layout[partner[:, None], first_slots[partner]])
    second_slots = second_moves.reshape(NDEV, M)
    partner = device_ids ^ N_GZ
    layout = layout.at[device_ids[:, None], second_slots].set(layout[partner[:, None], second_slots[partner]])
    return layout.reshape(-1)


def apply_all(field, operator, trace_index, owner_index):
    padded = jnp.pad(field, ((1, 1), (0, 0), (1, 1), (0, 0)))
    operator = operator.reshape(NDEV, E_DEV, W, K)
    reads = trace_index.reshape(NDEV, E_DEV, K)
    writes = owner_index.reshape(NDEV, E_DEV, K)
    def one_device(device):
        ix = device // (N_GY * N_GZ)
        iy = (device // N_GZ) % N_GY
        iz = device % N_GZ
        block = lax.dynamic_slice(padded, (ix * FX, iy, iz * FZ, jnp.int32(0)), (FX + 2, 1, FZ + 2, R))
        flattened = block.reshape((FX + 2) * (FZ + 2), R)
        gathered = flattened[reads[device]].astype(jnp.float32)
        local_ops = operator[device].astype(jnp.float32)
        tested = jnp.einsum('ewk,ekr->ewr', local_ops, gathered).astype(jnp.bfloat16)
        element_out = jnp.einsum('ewk,ewr->ekr', local_ops, tested.astype(jnp.float32))
        result = jnp.zeros((FX * FZ, R), jnp.float32).at[writes[device].reshape(-1)].add(element_out.reshape(-1, R))
        return result
    blocks = lax.map(one_device, jnp.arange(NDEV, dtype=jnp.int32))
    blocks = blocks.reshape(N_GX, N_GY, N_GZ, FX, FZ, R).transpose(0, 3, 1, 2, 4, 5)
    return blocks.reshape(N_GX * FX, N_GY, N_GZ * FZ, R)


def reference(gram_factor, coupling, order_class, first_moves, second_moves, trace_index, owner_index, traces):
    operator = element_products(gram_factor, coupling, order_class)
    operator = operator[relocate(first_moves, second_moves)]
    first = apply_all(traces, operator, trace_index, owner_index).astype(jnp.bfloat16)
    return apply_all(first, operator, trace_index, owner_index)
```

```python
import jax
import jax.numpy as jnp
from jax import lax
from jax.sharding import PartitionSpec as P


def swapped(block, axis, bit):
    count = lax.axis_size(axis)
    route = []
    for low in range(count):
        high = low | 1 << bit
        if high != low and high < count:
            route += [(low, high), (high, low)]
    return lax.ppermute(block, axis, route)


def with_halo(block, sides, width):
    for axis, dim in sides:
        count = lax.axis_size(axis)
        forward = [(i, i + 1) for i in range(count - 1)]
        backward = [(target, source) for source, target in forward]
        low = lax.ppermute(
            lax.slice_in_dim(block, block.shape[dim] - width, None, axis=dim), axis, forward
        )
        high = lax.ppermute(lax.slice_in_dim(block, 0, width, axis=dim), axis, backward)
        block = jnp.concatenate([low, block, high], axis=dim)
    return block


def product_of(masked, coupling):
    return jnp.einsum("ewv,evk->ewk", masked, coupling, preferred_element_type=jnp.float32).astype(
        jnp.bfloat16
    )


def picked(slots, operator):
    chosen = slots[:, None] == jnp.arange(operator.shape[0])[None, :]
    return jnp.einsum(
        "is,swk->iwk", chosen.astype(operator.dtype), operator, preferred_element_type=jnp.float32
    ).astype(operator.dtype)


def placed(operator, slots, arrived):
    numbers = jnp.arange(operator.shape[0])
    for i in range(slots.shape[0]):
        operator = jnp.where((numbers == slots[i])[:, None, None], arrived[i], operator)
    return operator


def body(
    gram_factor, coupling, order_class, first_moves, second_moves, trace_index, owner_index, traces
):
    width_full = gram_factor.shape[1]
    rows = lax.broadcasted_iota(jnp.int32, (1, width_full), 1)
    widths = width_full * (2 + order_class) // 4
    keep = (rows < widths[:, None]).astype(gram_factor.dtype)
    masked = gram_factor * keep[:, :, None]
    second_bit = lax.axis_size("gz").bit_length() - 1
    operator = product_of(masked, coupling)
    given = swapped(picked(first_moves, operator), "gz", 0)
    before = swapped(picked(second_moves, operator), ("gy", "gz"), second_bit)
    matches = second_moves[:, None] == first_moves[None, :]
    flagged = jnp.any(matches, axis=1).astype(jnp.bfloat16)
    patch = jnp.einsum(
        "ij,jwk->iwk", matches.astype(jnp.bfloat16), given, preferred_element_type=jnp.float32
    ).astype(jnp.bfloat16)
    patch_in, flag_in = swapped((patch, flagged), ("gy", "gz"), second_bit)
    given_two = jnp.where(flag_in[:, None, None] > 0.5, patch_in, before)
    operator = placed(operator, first_moves, given)
    operator = placed(operator, second_moves, given_two)
    rows_x = traces.shape[0]
    rows_z = traces.shape[2]
    columns = traces.shape[3]
    own_cells = lax.broadcasted_iota(jnp.int32, (1, rows_x * rows_z), 1)
    into = (owner_index.reshape(-1, 1) == own_cells).astype(jnp.bfloat16)
    cells = lax.broadcasted_iota(jnp.int32, (1, (rows_x + 2) * (rows_z + 2)), 1)
    reads = (trace_index.reshape(-1, 1) == cells).astype(jnp.bfloat16)
    slots, taken = trace_index.shape
    scattered = jnp.einsum(
        "ewk,ekn->ewn", operator, into.reshape(slots, taken, -1),
        preferred_element_type=jnp.float32,
    ).astype(jnp.bfloat16)

    def apply_field(field):
        extended = with_halo(field, (("gx", 0), ("gz", 1)), 1)
        flattened = extended.reshape(-1, columns)
        gathered = jnp.dot(reads, flattened, preferred_element_type=jnp.float32)
        gathered = gathered.astype(jnp.bfloat16).reshape(slots, taken, columns)
        tested = jnp.einsum(
            "ewk,ekr->ewr", operator, gathered, preferred_element_type=jnp.float32
        ).astype(jnp.bfloat16)
        result = jnp.einsum(
            "ewn,ewr->nr", scattered, tested, preferred_element_type=jnp.float32
        )
        return result.reshape(rows_x, rows_z, columns)

    first = apply_field(traces[:, 0]).astype(jnp.bfloat16)
    second = apply_field(first)
    return second[:, None]


def solution(mesh):
    return jax.shard_map(
        body,
        mesh=mesh,
        in_specs=(
            P(("gx", "gy", "gz"), None, None),
            P(("gx", "gy", "gz"), None, None),
            P(("gx", "gy", "gz")),
            P(("gx", "gy", "gz")),
            P(("gx", "gy", "gz")),
            P(("gx", "gy", "gz"), None),
            P(("gx", "gy", "gz"), None),
            P("gx", "gy", "gz", None),
        ),
        out_specs=P("gx", "gy", "gz", None),
        check_vma=False,
    )
```

```python
import functools

import jax
import jax.numpy as jnp
from jax import lax
from jax.experimental import pallas as pl
from jax.experimental.pallas import tpu as pltpu
from jax.sharding import PartitionSpec as P

MESH = pl.DeviceIdType.MESH
F32 = jnp.float32
BF16 = jnp.bfloat16


def product(left, right, dims=((1,), (0,))):
    return lax.dot_general(left, right, (dims, ((), ())), preferred_element_type=F32)


def other(index):
    return index + 1 - 2 * lax.rem(index, 2)


def kernel(
    sizes,
    gram_hbm,
    coupling,
    order_class,
    first_moves,
    second_moves,
    trace_index,
    owner_index,
    traces,
    out,
    gram,
    stage_one,
    stage_two,
    recv_one,
    recv_two,
    final,
    reads_own,
    reads_halo,
    into,
    scattered,
    gathered,
    tested,
    field,
    ends_one,
    ends_two,
    halo_one,
    halo_two,
    gram_sem,
    send_one,
    arrive_one,
    send_two,
    arrive_two,
    halo_send,
    halo_arrive,
    *local,
):
    rows_x, rows_z, count_x, count_z, part = sizes
    slots, width, _ = gram.shape
    taken = coupling.shape[2]
    cells = rows_x * rows_z
    moved = stage_one.shape[1]
    parts = width // part
    ix = lax.axis_index("gx")
    iy = lax.axis_index("gy")
    iz = lax.axis_index("gz")

    loads = []
    for c in range(parts):
        span = pl.ds(c * part, part)
        load = pltpu.make_async_copy(
            gram_hbm.at[:, span, :], gram.at[:, span, :], gram_sem.at[c]
        )
        load.start()
        loads.append(load)
    halo_one[...] = jnp.zeros_like(halo_one)
    halo_two[...] = jnp.zeros_like(halo_two)

    sides = (
        (ix > 0, {"gx": ix - 1}),
        (ix < count_x - 1, {"gx": ix + 1}),
        (iz > 0, {"gz": iz - 1}),
        (iz < count_z - 1, {"gz": iz + 1}),
    )
    barrier = pltpu.get_barrier_semaphore()
    partners = ({"gz": other(iz)}, {"gy": other(iy)})
    pl.semaphore_signal(barrier, inc=1, device_id=partners[1], device_id_type=MESH)
    peers = jnp.int32(1)
    for there, device in sides:
        peers += jnp.where(there, 1, 0)

        @pl.when(there)
        def _():
            pl.semaphore_signal(barrier, inc=1, device_id=device, device_id_type=MESH)

    end_rows = lax.broadcasted_iota(jnp.int32, (2 * rows_x, cells), 0)
    end_cells = lax.broadcasted_iota(jnp.int32, (2 * rows_x, cells), 1)
    wanted = jnp.where(
        end_rows < rows_x, end_rows * rows_z, (end_rows - rows_x) * rows_z + rows_z - 1
    )
    ends_pick = jnp.where(wanted == end_cells, 1.0, 0.0).astype(BF16)

    line = lax.broadcasted_iota(jnp.int32, (part, taken), 0)

    def operator_part(c):
        loads[c].wait()
        for s in range(slots):
            limit = width * (2 + order_class[s]) // 4
            made = product(gram[s, c * part : (c + 1) * part, :], coupling[s])
            kept = jnp.where(line + c * part < limit, made, 0.0)
            local[c][s] = kept.astype(BF16)

    def round_one(c):
        return pltpu.make_async_remote_copy(
            src_ref=stage_one.at[c],
            dst_ref=recv_one.at[c],
            send_sem=send_one.at[c],
            recv_sem=arrive_one.at[c],
            device_id=partners[0],
            device_id_type=MESH,
        )

    def round_two(c):
        return pltpu.make_async_remote_copy(
            src_ref=stage_two.at[c],
            dst_ref=recv_two.at[c],
            send_sem=send_two.at[c],
            recv_sem=arrive_two.at[c],
            device_id=partners[1],
            device_id_type=MESH,
        )

    def halo_copies(number, block, ends, halo):
        sources = (
            block.at[pl.ds(0, rows_z)],
            block.at[pl.ds(cells - rows_z, rows_z)],
            ends.at[pl.ds(0, rows_x)],
            ends.at[pl.ds(rows_x, rows_x)],
        )
        copies = []
        for k, (there, device) in enumerate(sides):
            place = k + 1 - 2 * (k % 2)
            copies.append(
                pltpu.make_async_remote_copy(
                    src_ref=sources[k],
                    dst_ref=halo.at[place],
                    send_sem=halo_send.at[number, k],
                    recv_sem=halo_arrive.at[number, place],
                    device_id=device,
                    device_id_type=MESH,
                )
            )
        return copies

    def halo_start(copies):
        for (there, _), copy in zip(sides, copies):
            pl.when(there)(copy.start)

    def halo_wait(copies):
        for k, (there, _) in enumerate(sides):
            pl.when(there)(copies[k + 1 - 2 * (k % 2)].wait_recv)

    def halo_sent(copies):
        for (there, _), copy in zip(sides, copies):
            pl.when(there)(copy.wait_send)

    ends_one[...] = product(ends_pick, traces[...]).astype(BF16)
    operator_part(0)
    for i in range(moved):
        stage_one[0, i] = local[0][first_moves[i]]

    pl.semaphore_wait(barrier, peers)
    halos_one = halo_copies(0, traces, ends_one, halo_one)
    halo_start(halos_one)
    round_one(0).start()
    for c in range(1, parts):
        operator_part(c)
        for i in range(moved):
            stage_one[c, i] = local[c][first_moves[i]]
        round_one(c).start()

    wide = rows_z + 2
    number = trace_index[...]
    a = (number * (-(-65536 // wide))) >> 16
    b = number - a * wide
    cell = (a - 1) * rows_z + b - 1
    cell = jnp.where(a == 0, cells + b - 1, cell)
    cell = jnp.where(a == rows_x + 1, cells + rows_z + b - 1, cell)
    cell = jnp.where(b == 0, cells + 2 * rows_z + a - 1, cell)
    cell = jnp.where(b == rows_z + 1, cells + 2 * rows_z + rows_x + a - 1, cell)
    square = jnp.concatenate(
        [cell.astype(F32), jnp.zeros((taken - slots, taken), F32)], axis=0
    )
    upright = square.T.astype(jnp.int32)
    frame = halo_one.shape[0] * halo_one.shape[1]
    lane_own = lax.broadcasted_iota(jnp.int32, (taken, cells), 1)
    lane_halo = lax.broadcasted_iota(jnp.int32, (taken, frame), 1) + cells
    row_own = lax.broadcasted_iota(jnp.int32, (cells, taken), 0)

    def pick(s):
        column = upright[:, s : s + 1]
        reads_own[s] = jnp.where(column == lane_own, 1.0, 0.0).astype(BF16)
        reads_halo[s] = jnp.where(column == lane_halo, 1.0, 0.0).astype(BF16)

    def spread(s):
        into[s] = jnp.where(row_own == owner_index[s : s + 1, :], 1.0, 0.0).astype(BF16)

    def pass_on(c):
        round_one(c).wait_recv()
        for j in range(moved):
            value = local[c][second_moves[j]]
            for i in range(moved):
                value = jnp.where(second_moves[j] == first_moves[i], recv_one[c, i], value)
            stage_two[c, j] = value
        round_two(c).start()

    for s in range(slots):
        pick(s)
    for s in range(slots):
        gathered[s] = product(reads_own[s], traces[...]).astype(BF16)
    pass_on(0)
    for s in range(slots):
        spread(s)
    halo_wait(halos_one)

    def gather_halo(halo):
        rows = halo[...].reshape(frame, halo.shape[2])
        for s in range(slots):
            gathered[s] += product(reads_halo[s], rows).astype(BF16)

    gather_halo(halo_one)
    for c in range(1, parts):
        pass_on(c)

    total = jnp.zeros((cells, traces.shape[1]), F32)
    for c in range(parts):
        span = slice(c * part, (c + 1) * part)
        round_two(c).wait_recv()
        for s in range(slots):
            value = local[c][s]
            for i in range(moved):
                value = jnp.where(first_moves[i] == s, recv_one[c, i], value)
            for j in range(moved):
                value = jnp.where(second_moves[j] == s, recv_two[c, j], value)
            final[s, span, :] = value
        for s in range(slots):
            scattered[s, :, span] = product(
                into[s], final[s, span, :], ((1,), (1,))
            ).astype(BF16)
            tested[s, span, :] = product(final[s, span, :], gathered[s]).astype(BF16)
        for s in range(slots):
            total += product(scattered[s, :, span], tested[s, span, :])
    field[...] = total.astype(BF16)

    ends_two[...] = product(ends_pick, field[...]).astype(BF16)
    halos_two = halo_copies(1, field, ends_two, halo_two)
    halo_start(halos_two)
    for s in range(slots):
        gathered[s] = product(reads_own[s], field[...]).astype(BF16)
    halo_wait(halos_two)
    gather_halo(halo_two)
    total = jnp.zeros((cells, traces.shape[1]), F32)
    for s in range(slots):
        tested[s] = product(final[s], gathered[s]).astype(BF16)
        total += product(scattered[s], tested[s])
    out[...] = total
    for c in range(parts):
        round_one(c).wait_send()
        round_two(c).wait_send()
    halo_sent(halos_one)
    halo_sent(halos_two)


def body(
    gram_factor, coupling, order_class, first_moves, second_moves, trace_index, owner_index, traces
):
    slots, width, _ = gram_factor.shape
    taken = coupling.shape[2]
    rows_x, _, rows_z, columns = traces.shape
    cells = rows_x * rows_z
    moved = first_moves.shape[0]
    part = 128
    parts = width // part
    sizes = (rows_x, rows_z, lax.axis_size("gx"), lax.axis_size("gz"), part)
    vmem = pl.BlockSpec(memory_space=pltpu.VMEM)
    smem = pl.BlockSpec(memory_space=pltpu.SMEM)
    moving = pltpu.VMEM((parts, moved, part, taken), BF16)
    halo = pltpu.VMEM((4, rows_z, columns), BF16)
    ends = pltpu.VMEM((2 * rows_x, columns), BF16)
    result = pl.pallas_call(
        functools.partial(kernel, sizes),
        out_shape=jax.ShapeDtypeStruct((cells, columns), F32),
        in_specs=[pl.BlockSpec(memory_space=pl.ANY), vmem, smem, smem, smem, vmem, vmem, vmem],
        out_specs=vmem,
        scratch_shapes=[
            pltpu.VMEM((slots, width, width), BF16),
            moving,
            moving,
            moving,
            moving,
            pltpu.VMEM((slots, width, taken), BF16),
            pltpu.VMEM((slots, taken, cells), BF16),
            pltpu.VMEM((slots, taken, 2 * (rows_x + rows_z)), BF16),
            pltpu.VMEM((slots, cells, taken), BF16),
            pltpu.VMEM((slots, cells, width), BF16),
            pltpu.VMEM((slots, taken, columns), BF16),
            pltpu.VMEM((slots, width, columns), BF16),
            pltpu.VMEM((cells, columns), BF16),
            ends,
            ends,
            halo,
            halo,
            pltpu.SemaphoreType.DMA((parts,)),
            pltpu.SemaphoreType.DMA((parts,)),
            pltpu.SemaphoreType.DMA((parts,)),
            pltpu.SemaphoreType.DMA((parts,)),
            pltpu.SemaphoreType.DMA((parts,)),
            pltpu.SemaphoreType.DMA((2, 4)),
            pltpu.SemaphoreType.DMA((2, 4)),
        ]
        + [pltpu.VMEM((slots, part, taken), BF16)] * parts,
        compiler_params=pltpu.CompilerParams(
            collective_id=0, has_side_effects=True, vmem_limit_bytes=48 * 1024 * 1024
        ),
    )(
        gram_factor,
        coupling,
        order_class,
        first_moves,
        second_moves,
        trace_index,
        owner_index,
        traces.reshape(cells, columns),
    )
    return result.reshape(traces.shape)


def solution(mesh):
    return jax.shard_map(
        body,
        mesh=mesh,
        in_specs=(
            P(("gx", "gy", "gz"), None, None),
            P(("gx", "gy", "gz"), None, None),
            P(("gx", "gy", "gz")),
            P(("gx", "gy", "gz")),
            P(("gx", "gy", "gz")),
            P(("gx", "gy", "gz"), None),
            P(("gx", "gy", "gz"), None),
            P("gx", "gy", "gz", None),
        ),
        out_specs=P("gx", "gy", "gz", None),
        check_vma=False,
    )
```

```python
import functools

import jax
import jax.numpy as jnp
from jax import lax
from jax.experimental import pallas as pl
from jax.experimental.pallas import tpu as pltpu
from jax.sharding import PartitionSpec as P

MESH = pl.DeviceIdType.MESH
F32 = jnp.float32
BF16 = jnp.bfloat16


def product(left, right, dims=((1,), (0,))):
    return lax.dot_general(left, right, (dims, ((), ())), preferred_element_type=F32)


def other(index):
    return index + 1 - 2 * lax.rem(index, 2)


def kernel(
    sizes,
    gram_hbm,
    coupling_hbm,
    order_class_hbm,
    first_moves_hbm,
    second_moves_hbm,
    trace_index_hbm,
    owner_index_hbm,
    traces_hbm,
    out,
    gram,
    coupling,
    order_class,
    first_moves,
    second_moves,
    trace_index,
    owner_index,
    traces,
    input_sem,
    stage_one,
    stage_two,
    recv_one,
    recv_two,
    final,
    reads_own,
    reads_halo,
    into,
    scattered,
    gathered,
    tested,
    field,
    ends_one,
    ends_two,
    halo_one,
    halo_two,
    gram_sem,
    send_one,
    arrive_one,
    send_two,
    arrive_two,
    halo_send,
    halo_arrive,
    *local,
):
    rows_x, rows_z, count_x, count_z, part, group = sizes
    slots, width, _ = gram.shape
    taken = coupling.shape[2]
    cells = rows_x * rows_z
    moved = stage_one.shape[1]
    parts = width // part
    ix = lax.axis_index("gx")
    iy = lax.axis_index("gy")
    iz = lax.axis_index("gz")

    inputs = []
    for n, (source, held) in enumerate(
        (
            (coupling_hbm, coupling),
            (order_class_hbm, order_class),
            (first_moves_hbm, first_moves),
            (second_moves_hbm, second_moves),
            (traces_hbm, traces),
            (trace_index_hbm, trace_index),
            (owner_index_hbm, owner_index),
        )
    ):
        load = pltpu.make_async_copy(source, held, input_sem.at[n])
        load.start()
        inputs.append(load)
    loads = []
    for c in range(parts):
        span = pl.ds(c * part, part)
        load = pltpu.make_async_copy(
            gram_hbm.at[:, span, :], gram.at[:, span, :], gram_sem.at[c]
        )
        load.start()
        loads.append(load)
    halo_one[...] = jnp.zeros_like(halo_one)
    halo_two[...] = jnp.zeros_like(halo_two)

    sides = (
        (ix > 0, {"gx": ix - 1}),
        (ix < count_x - 1, {"gx": ix + 1}),
        (iz > 0, {"gz": iz - 1}),
        (iz < count_z - 1, {"gz": iz + 1}),
    )
    barrier = pltpu.get_barrier_semaphore()
    partners = ({"gz": other(iz)}, {"gy": other(iy)})
    pl.semaphore_signal(barrier, inc=1, device_id=partners[1], device_id_type=MESH)
    peers = jnp.int32(1)
    for there, device in sides:
        peers += jnp.where(there, 1, 0)

        @pl.when(there)
        def _():
            pl.semaphore_signal(barrier, inc=1, device_id=device, device_id_type=MESH)

    end_rows = lax.broadcasted_iota(jnp.int32, (2 * rows_x, cells), 0)
    end_cells = lax.broadcasted_iota(jnp.int32, (2 * rows_x, cells), 1)
    wanted = jnp.where(
        end_rows < rows_x, end_rows * rows_z, (end_rows - rows_x) * rows_z + rows_z - 1
    )
    ends_pick = jnp.where(wanted == end_cells, 1.0, 0.0).astype(BF16)

    line = lax.broadcasted_iota(jnp.int32, (part, taken), 0)

    def operator_part(c):
        loads[c].wait()
        for s in range(slots):
            limit = width * (2 + order_class[s]) // 4
            made = product(gram[s, c * part : (c + 1) * part, :], coupling[s])
            kept = jnp.where(line + c * part < limit, made, 0.0)
            local[c][s] = kept.astype(BF16)

    def round_one(c):
        return pltpu.make_async_remote_copy(
            src_ref=stage_one.at[c],
            dst_ref=recv_one.at[c],
            send_sem=send_one.at[c],
            recv_sem=arrive_one.at[c],
            device_id=partners[0],
            device_id_type=MESH,
        )

    def round_two(c):
        return pltpu.make_async_remote_copy(
            src_ref=stage_two.at[c],
            dst_ref=recv_two.at[c],
            send_sem=send_two.at[c],
            recv_sem=arrive_two.at[c],
            device_id=partners[1],
            device_id_type=MESH,
        )

    def halo_copies(number, block, ends, halo):
        sources = (
            block.at[pl.ds(0, rows_z)],
            block.at[pl.ds(cells - rows_z, rows_z)],
            ends.at[pl.ds(0, rows_x)],
            ends.at[pl.ds(rows_x, rows_x)],
        )
        copies = []
        for k, (there, device) in enumerate(sides):
            place = k + 1 - 2 * (k % 2)
            copies.append(
                pltpu.make_async_remote_copy(
                    src_ref=sources[k],
                    dst_ref=halo.at[place],
                    send_sem=halo_send.at[number, k],
                    recv_sem=halo_arrive.at[number, place],
                    device_id=device,
                    device_id_type=MESH,
                )
            )
        return copies

    def halo_start(copies):
        for (there, _), copy in zip(sides, copies):
            pl.when(there)(copy.start)

    def halo_wait(copies):
        for k, (there, _) in enumerate(sides):
            pl.when(there)(copies[k + 1 - 2 * (k % 2)].wait_recv)

    def halo_sent(copies):
        for (there, _), copy in zip(sides, copies):
            pl.when(there)(copy.wait_send)

    for load in inputs:
        load.wait()
    ends_one[...] = product(ends_pick, traces[...]).astype(BF16)
    operator_part(0)
    for i in range(moved):
        stage_one[0, i] = local[0][first_moves[i]]

    pl.semaphore_wait(barrier, peers)
    halos_one = halo_copies(0, traces, ends_one, halo_one)
    halo_start(halos_one)
    round_one(0).start()
    for c in range(1, parts):
        operator_part(c)
        for i in range(moved):
            stage_one[c, i] = local[c][first_moves[i]]
        round_one(c).start()

    wide = rows_z + 2
    number = trace_index[...]
    a = (number * (-(-65536 // wide))) >> 16
    b = number - a * wide
    cell = (a - 1) * rows_z + b - 1
    cell = jnp.where(a == 0, cells + b - 1, cell)
    cell = jnp.where(a == rows_x + 1, cells + rows_z + b - 1, cell)
    cell = jnp.where(b == 0, cells + 2 * rows_z + a - 1, cell)
    cell = jnp.where(b == rows_z + 1, cells + 2 * rows_z + rows_x + a - 1, cell)
    square = jnp.concatenate(
        [cell.astype(F32), jnp.zeros((taken - slots, taken), F32)], axis=0
    )
    upright = square.T.astype(jnp.int32)
    frame = halo_one.shape[0] * halo_one.shape[1]
    lane_own = lax.broadcasted_iota(jnp.int32, (taken, cells), 1)
    lane_halo = lax.broadcasted_iota(jnp.int32, (taken, frame), 1) + cells
    row_own = lax.broadcasted_iota(jnp.int32, (cells, taken), 0)

    def pick(s):
        column = upright[:, s : s + 1]
        reads_own[s] = jnp.where(column == lane_own, 1.0, 0.0).astype(BF16)
        reads_halo[s] = jnp.where(column == lane_halo, 1.0, 0.0).astype(BF16)

    def spread(s):
        into[s] = jnp.where(row_own == owner_index[s : s + 1, :], 1.0, 0.0).astype(BF16)

    def pass_on(c):
        round_one(c).wait_recv()
        for j in range(moved):
            value = local[c][second_moves[j]]
            for i in range(moved):
                value = jnp.where(second_moves[j] == first_moves[i], recv_one[c, i], value)
            stage_two[c, j] = value
        round_two(c).start()

    for s in range(slots):
        pick(s)
    for s in range(slots):
        gathered[s] = product(reads_own[s], traces[...]).astype(BF16)
    pass_on(0)
    for s in range(slots):
        spread(s)
    halo_wait(halos_one)

    def gather_halo(halo):
        rows = halo[...].reshape(frame, halo.shape[2])
        for s in range(slots):
            gathered[s] += product(reads_halo[s], rows).astype(BF16)

    gather_halo(halo_one)
    for c in range(1, parts):
        pass_on(c)

    total = jnp.zeros((cells, traces.shape[1]), F32)
    for first in range(0, parts, group):
        for c in range(first, first + group):
            round_two(c).wait_recv()
            for s in range(slots):
                value = local[c][s]
                for i in range(moved):
                    value = jnp.where(first_moves[i] == s, recv_one[c, i], value)
                for j in range(moved):
                    value = jnp.where(second_moves[j] == s, recv_two[c, j], value)
                final[s, c * part : (c + 1) * part, :] = value
        span = slice(first * part, (first + group) * part)
        for s in range(slots):
            scattered[s, :, span] = product(
                into[s], final[s, span, :], ((1,), (1,))
            ).astype(BF16)
            tested[s, span, :] = product(final[s, span, :], gathered[s]).astype(BF16)
        for s in range(slots):
            total += product(scattered[s, :, span], tested[s, span, :])
    field[...] = total.astype(BF16)

    ends_two[...] = product(ends_pick, field[...]).astype(BF16)
    halos_two = halo_copies(1, field, ends_two, halo_two)
    halo_start(halos_two)
    for s in range(slots):
        gathered[s] = product(reads_own[s], field[...]).astype(BF16)
    halo_wait(halos_two)
    gather_halo(halo_two)
    total = jnp.zeros((cells, traces.shape[1]), F32)
    for s in range(slots):
        tested[s] = product(final[s], gathered[s]).astype(BF16)
        total += product(scattered[s], tested[s])
    out[...] = total
    for c in range(parts):
        round_one(c).wait_send()
        round_two(c).wait_send()
    halo_sent(halos_one)
    halo_sent(halos_two)


def body(
    gram_factor, coupling, order_class, first_moves, second_moves, trace_index, owner_index, traces
):
    slots, width, _ = gram_factor.shape
    taken = coupling.shape[2]
    rows_x, _, rows_z, columns = traces.shape
    cells = rows_x * rows_z
    moved = first_moves.shape[0]
    part = 64
    parts = width // part
    sizes = (rows_x, rows_z, lax.axis_size("gx"), lax.axis_size("gz"), part, 2)
    vmem = pl.BlockSpec(memory_space=pltpu.VMEM)
    moving = pltpu.VMEM((parts, moved, part, taken), BF16)
    halo = pltpu.VMEM((4, rows_z, columns), BF16)
    ends = pltpu.VMEM((2 * rows_x, columns), BF16)
    result = pl.pallas_call(
        functools.partial(kernel, sizes),
        out_shape=jax.ShapeDtypeStruct((cells, columns), F32),
        in_specs=[pl.BlockSpec(memory_space=pltpu.HBM)] * 8,
        out_specs=vmem,
        scratch_shapes=[
            pltpu.VMEM((slots, width, width), BF16),
            pltpu.VMEM(coupling.shape, BF16),
            pltpu.SMEM(order_class.shape, jnp.int32),
            pltpu.SMEM(first_moves.shape, jnp.int32),
            pltpu.SMEM(second_moves.shape, jnp.int32),
            pltpu.VMEM(trace_index.shape, jnp.int32),
            pltpu.VMEM(owner_index.shape, jnp.int32),
            pltpu.VMEM((cells, columns), BF16),
            pltpu.SemaphoreType.DMA((7,)),
            moving,
            moving,
            moving,
            moving,
            pltpu.VMEM((slots, width, taken), BF16),
            pltpu.VMEM((slots, taken, cells), BF16),
            pltpu.VMEM((slots, taken, 2 * (rows_x + rows_z)), BF16),
            pltpu.VMEM((slots, cells, taken), BF16),
            pltpu.VMEM((slots, cells, width), BF16),
            pltpu.VMEM((slots, taken, columns), BF16),
            pltpu.VMEM((slots, width, columns), BF16),
            pltpu.VMEM((cells, columns), BF16),
            ends,
            ends,
            halo,
            halo,
            pltpu.SemaphoreType.DMA((parts,)),
            pltpu.SemaphoreType.DMA((parts,)),
            pltpu.SemaphoreType.DMA((parts,)),
            pltpu.SemaphoreType.DMA((parts,)),
            pltpu.SemaphoreType.DMA((parts,)),
            pltpu.SemaphoreType.DMA((2, 4)),
            pltpu.SemaphoreType.DMA((2, 4)),
        ]
        + [pltpu.VMEM((slots, part, taken), BF16)] * parts,
        compiler_params=pltpu.CompilerParams(
            collective_id=0, has_side_effects=True, vmem_limit_bytes=61 * 1024 * 1024
        ),
    )(
        gram_factor,
        coupling,
        order_class,
        first_moves,
        second_moves,
        trace_index,
        owner_index,
        traces.reshape(cells, columns),
    )
    return result.reshape(traces.shape)


def solution(mesh):
    return jax.shard_map(
        body,
        mesh=mesh,
        in_specs=(
            P(("gx", "gy", "gz"), None, None),
            P(("gx", "gy", "gz"), None, None),
            P(("gx", "gy", "gz")),
            P(("gx", "gy", "gz")),
            P(("gx", "gy", "gz")),
            P(("gx", "gy", "gz"), None),
            P(("gx", "gy", "gz"), None),
            P("gx", "gy", "gz", None),
        ),
        out_specs=P("gx", "gy", "gz", None),
        check_vma=False,
    )
```
